32 devices in a mesh: row: 8 (over z, y), col: 4 (over x, core).
Axes of the slice: x: 2, y: 2, z: 4, core: 2. Of those that a mesh axis runs over, the one named last changes fastest.
Arguments:
- covariance: float32 [16384, 16384], P('row', 'col'), as said below
- courant: float32 [2, 16384], replicated, may hold values from 0.05 to 0.45
- upwind: int32 [16384], replicated, may hold values from 0 to 3
- observed: int32 [2, 256], replicated, may hold values from 0 to 16383
- noise: float32 [2, 256], replicated, may hold values from 0.5 to 2
Outputs:
- posterior: float32 [16384, 16384], P('row', 'col')
The draws below stay inside these ranges and needn't reach their ends.
Inputs may be any that keep to these rules, and one draw needn't show every extreme that they name: The covariance is symmetric and positive definite.
All inputs are finite; a program needn't handle non-finite values.
Results may differ from the reference program's by a relative error of at most 0.0003.
Values sent between devices are 32-bit elements; how exact they have to be, the bound alone decides.
A program may use at most 256 MiB of HBM per device.

```python
import math
import jax
import jax.numpy as jnp
from jax import lax

G = 128
KOBS = 256
BATCHES = 2
NC = 16384


def smooth_fields(white, lengths):
    base = jnp.arange(G, dtype=jnp.float32)
    spacing = base[:, None] - base[None, :]
    kernels = jnp.exp(-spacing[None, :, :] ** 2 / (2.0 * lengths[:, None, None] ** 2))
    first = jnp.einsum('jab,jbc->jac', kernels, white, precision=lax.Precision.HIGHEST)
    fields = jnp.einsum('jac,jdc->jad', first, kernels, precision=lax.Precision.HIGHEST)
    spread = jnp.sqrt(jnp.mean(fields * fields, axis=(1, 2), keepdims=True) + 1e-12)
    return fields / spread


def draw_covariance(key, part):
    total = G * G
    count = min(2048, total)
    keys = jax.random.split(jax.random.fold_in(key, 7), 4)
    white = jax.random.normal(keys[0], (count, G, G), jnp.float32)
    lengths = jnp.exp(jax.random.uniform(keys[1], (count,), jnp.float32, math.log(max(1.0, G / 32.0)), math.log(G / 4.0)))
    amplitude = jnp.exp(jax.random.uniform(keys[2], (total,), jnp.float32, math.log(0.5), math.log(2.0)))
    floor_vals = jnp.exp(jax.random.uniform(keys[3], (total,), jnp.float32, math.log(0.25), math.log(1.0)))
    fields = smooth_fields(white, lengths)
    basis = fields.reshape(count, total) * amplitude[None, :]
    gram = jnp.dot(basis.T, basis, precision=lax.Precision.HIGHEST, preferred_element_type=jnp.float32) / count
    gram = 0.5 * (gram + gram.T)
    cells = jnp.arange(total)
    return gram.at[cells, cells].add(floor_vals)


def touch_ends(result, stream_key, smallest, largest):
    spot = [jax.random.randint(jax.random.fold_in(stream_key, axis), (), 0, length) for axis, length in enumerate(result.shape)]
    main_axis = result.shape.index(max(result.shape))
    neighbour = spot[:main_axis] + [(spot[main_axis] + 1) % result.shape[main_axis]] + spot[main_axis + 1:]
    return result.at[tuple(spot)].set(smallest).at[tuple(neighbour)].set(largest)


def setup_inputs(seed: int = 0) -> dict:
    seeds = jax.random.split(jax.random.key(seed), 6)
    return {
        "covariance": draw_covariance(jax.random.fold_in(seeds[5], 71), 0),
        "courant": jnp.clip(jax.random.uniform(seeds[1], (2, NC), jnp.float32, 0.05, 0.45), 0.05, 0.45),
        "upwind": touch_ends(jax.random.randint(seeds[2], (NC,), 0, 4), jax.random.fold_in(seeds[2], 1), 0, 3).astype(jnp.int32),
        "observed": touch_ends(jax.random.randint(seeds[3], (BATCHES, KOBS), 0, NC), jax.random.fold_in(seeds[3], 1), 0, NC - 1).astype(jnp.int32),
        "noise": jnp.clip(jnp.exp(jax.random.uniform(seeds[4], (BATCHES, KOBS), jnp.float32, math.log(0.5), math.log(2.0))), 0.5, 2.0),
    }


def left_apply(padded, cour_a, cour_b, up_dir):
    lines = padded.shape[0] - 2
    center = padded[1:-1]
    prev_line = padded[:-2]
    next_line = padded[2:]
    prev_cell = jnp.pad(center, ((0, 0), (1, 0), (0, 0)))[:, :-1]
    next_cell = jnp.pad(center, ((0, 0), (0, 1), (0, 0)))[:, 1:]
    coef_a = cour_a.reshape(lines, G, 1)
    coef_b = cour_b.reshape(lines, G, 1)
    dirs = up_dir.reshape(lines, G, 1)
    up_line = jnp.where(dirs % 2 == 1, next_line, prev_line)
    up_cell = jnp.where(dirs // 2 == 1, next_cell, prev_cell)
    return (1.0 - coef_a - coef_b) * center + coef_a * up_line + coef_b * up_cell

def right_apply(padded, cour_a, cour_b, up_dir):
    lines = padded.shape[1] - 2
    center = padded[:, 1:-1]
    prev_line = padded[:, :-2]
    next_line = padded[:, 2:]
    prev_cell = jnp.pad(center, ((0, 0), (0, 0), (1, 0)))[:, :, :-1]
    next_cell = jnp.pad(center, ((0, 0), (0, 0), (0, 1)))[:, :, 1:]
    coef_a = cour_a.reshape(1, lines, G)
    coef_b = cour_b.reshape(1, lines, G)
    dirs = up_dir.reshape(1, lines, G)
    up_line = jnp.where(dirs % 2 == 1, next_line, prev_line)
    up_cell = jnp.where(dirs // 2 == 1, next_cell, prev_cell)
    return (1.0 - coef_a - coef_b) * center + coef_a * up_line + coef_b * up_cell

def reference(covariance, courant, upwind, observed, noise):
    total = G * G
    state = covariance
    for cycle in range(BATCHES):
        padded = jnp.pad(state.reshape(G, G, total), ((1, 1), (0, 0), (0, 0)))
        state = left_apply(padded, courant[0], courant[1], upwind).reshape(total, total)
        padded = jnp.pad(state.reshape(total, G, G), ((0, 0), (1, 1), (0, 0)))
        state = right_apply(padded, courant[0], courant[1], upwind).reshape(total, total)
        obs = observed[cycle]
        col_panel = jnp.take(state, obs, axis=1)
        row_panel = jnp.take(state, obs, axis=0)
        innov = jnp.take(row_panel, obs, axis=1) + jnp.diag(noise[cycle])
        factor = jnp.linalg.cholesky(innov)
        gain = jax.scipy.linalg.cho_solve((factor, True), col_panel.T).T
        state = state - jnp.dot(gain.astype(jnp.float32), row_panel.astype(jnp.float32), precision=lax.Precision.HIGHEST, preferred_element_type=jnp.float32)
    return state
```

```python
import functools
import math

import jax
import jax.numpy as jnp
from jax import lax
from jax.experimental import pallas as pl
from jax.experimental.pallas import tpu as pltpu
from jax.sharding import PartitionSpec as P

VMEM_BYTES = 56 * 2**20
HIGHEST = lax.Precision.HIGHEST


def shifted(block, axis, dim, width):
    count = lax.axis_size(axis)
    forward = [(i, i + 1) for i in range(count - 1)]
    backward = [(target, source) for source, target in forward]
    size = block.shape[dim]
    low = lax.ppermute(lax.slice_in_dim(block, size - width, size, axis=dim), axis, forward)
    high = lax.ppermute(lax.slice_in_dim(block, 0, width, axis=dim), axis, backward)
    return low, high


def stencil(coefs, prev, center, following, axis, side):
    out = coefs[0] * center + coefs[1] * prev + coefs[2] * following
    out = out + coefs[3] * pltpu.roll(center, 1, axis)
    return out + coefs[4] * pltpu.roll(center, side - 1, axis)


def each_line(first, last, group, body):
    rounds = (last - first) // group

    @pl.loop(0, rounds)
    def _(turn):
        for place in range(group):
            body(first + turn * group + place)

    for line in range(first + rounds * group, last):
        body(line)


def sweep(side, lines, low, middle, high, coefs_at, half, store, axis, group):
    def first(line, prev, center, following):
        half(line + 1, stencil(coefs_at(line + 1), prev, center, following, axis, side))

    first(-1, low(0), low(1), middle(0))
    first(0, low(1), middle(0), middle(1))

    each_line(
        1,
        lines - 1,
        group,
        lambda line: first(line, middle(line - 1), middle(line), middle(line + 1)),
    )
    first(lines - 1, middle(lines - 2), middle(lines - 1), high(0))
    first(lines, middle(lines - 1), high(0), high(1))

    def second(line):
        out = stencil(coefs_at(line + 1), half(line), half(line + 1), half(line + 2), axis, side)
        store(line, out)

    each_line(0, lines, group, second)


def start_of(line, side):
    return pl.ds(line * side if isinstance(line, int) else pl.multiple_of(line * side, side), side)


def left_kernel(side, low_ref, mid_ref, high_ref, coef_ref, out_ref, half_ref):
    rows, width = mid_ref.shape
    lanes = coef_ref.shape[2]
    for piece in range(width // lanes):
        cols = pl.ds(piece * lanes, lanes)

        def read(ref):
            return lambda line: ref[start_of(line, side), cols]

        def half(line, value=None):
            if value is None:
                return half_ref[start_of(line, side), cols]
            half_ref[start_of(line, side), cols] = value

        def store(line, value):
            out_ref[start_of(line, side), cols] = value

        def coefs_at(line):
            return [coef_ref[k, start_of(line, side), :] for k in range(5)]

        sweep(side, rows // side, read(low_ref), read(mid_ref), read(high_ref), coefs_at, half, store, 0, 1)


def right_kernel(side, low_ref, mid_ref, high_ref, coef_ref, out_ref, half_ref):
    rows, width = mid_ref.shape
    copies = rows // coef_ref.shape[1]

    def read(ref):
        return lambda line: ref[:, start_of(line, side)]

    def half(line, value=None):
        if value is None:
            return half_ref[:, start_of(line, side)]
        half_ref[:, start_of(line, side)] = value

    def store(line, value):
        out_ref[:, start_of(line, side)] = value

    def coefs_at(line):
        return [
            jnp.concatenate([coef_ref[k, :, start_of(line, side)]] * copies, axis=0)
            for k in range(5)
        ]

    sweep(side, width // side, read(low_ref), read(mid_ref), read(high_ref), coefs_at, half, store, 1, 3)


def left_twice(low, block, high, coefs, side):
    rows, width = block.shape
    tile = min(256, width)
    lanes = 128
    spread = jnp.broadcast_to(coefs[:, :, None], (*coefs.shape, lanes))

    def spec(count):
        return pl.BlockSpec((count, tile), lambda i: (0, i))

    return pl.pallas_call(
        functools.partial(left_kernel, side),
        grid=(width // tile,),
        in_specs=[
            spec(2 * side),
            spec(rows),
            spec(2 * side),
            pl.BlockSpec(spread.shape, lambda i: (0, 0, 0)),
        ],
        out_specs=spec(rows),
        out_shape=jax.ShapeDtypeStruct(block.shape, block.dtype),
        scratch_shapes=[pltpu.VMEM((rows + 2 * side, tile), block.dtype)],
        compiler_params=pltpu.CompilerParams(vmem_limit_bytes=VMEM_BYTES),
        cost_estimate=pl.CostEstimate(
            flops=36 * rows * width, bytes_accessed=8 * rows * width, transcendentals=0
        ),
    )(low, block, high, spread)


def right_twice(low, block, high, coefs, side):
    rows, width = block.shape
    tile = min(128, rows)
    spread = jnp.broadcast_to(coefs[:, None, :], (coefs.shape[0], 8, coefs.shape[1]))

    def spec(count):
        return pl.BlockSpec((tile, count), lambda i: (i, 0))

    return pl.pallas_call(
        functools.partial(right_kernel, side),
        grid=(rows // tile,),
        in_specs=[
            spec(2 * side),
            spec(width),
            spec(2 * side),
            pl.BlockSpec(spread.shape, lambda i: (0, 0, 0)),
        ],
        out_specs=spec(width),
        out_shape=jax.ShapeDtypeStruct(block.shape, block.dtype),
        scratch_shapes=[pltpu.VMEM((tile, width + 2 * side), block.dtype)],
        compiler_params=pltpu.CompilerParams(vmem_limit_bytes=VMEM_BYTES),
        cost_estimate=pl.CostEstimate(
            flops=36 * rows * width, bytes_accessed=8 * rows * width, transcendentals=0
        ),
    )(low, block, high, spread)


def subtract_kernel(tile, block_ref, left_ref, right_ref, out_ref):
    @pl.loop(0, block_ref.shape[1] // tile)
    def _(turn):
        cols = pl.ds(pl.multiple_of(turn * tile, tile), tile)
        product = jnp.dot(
            left_ref[...],
            right_ref[:, cols],
            precision=HIGHEST,
            preferred_element_type=jnp.float32,
        )
        out_ref[:, cols] = block_ref[:, cols] - product


def subtract_product(block, left, right):
    rows, width = block.shape
    depth = left.shape[1]
    tile = min(256, rows)

    def strip(count):
        return pl.BlockSpec((tile, count), lambda i: (i, 0))

    return pl.pallas_call(
        functools.partial(subtract_kernel, min(512, width)),
        grid=(rows // tile,),
        in_specs=[strip(width), strip(depth), pl.BlockSpec((depth, width), lambda i: (0, 0))],
        out_specs=strip(width),
        out_shape=jax.ShapeDtypeStruct(block.shape, block.dtype),
        compiler_params=pltpu.CompilerParams(vmem_limit_bytes=VMEM_BYTES),
        cost_estimate=pl.CostEstimate(
            flops=12 * rows * width * depth, bytes_accessed=8 * rows * width, transcendentals=0
        ),
    )(block, left, right)


def stencil_coefs(courant, upwind, side):
    total = upwind.shape[0]
    place = jnp.arange(total) % side
    frac_a, frac_b = courant[0], courant[1]
    next_line, next_cell = upwind % 2 == 1, upwind // 2 == 1
    coefs = jnp.stack(
        [
            1.0 - frac_a - frac_b,
            jnp.where(next_line, 0.0, frac_a),
            jnp.where(next_line, frac_a, 0.0),
            jnp.where(next_cell | (place == 0), 0.0, frac_b),
            jnp.where(next_cell & (place != side - 1), frac_b, 0.0),
        ]
    )
    return jnp.pad(coefs, ((0, 0), (side, side)))


def expand(index, value, table, side):
    total = table.shape[1]
    frac_a, frac_b, dirs = jnp.take(table, index.reshape(-1), axis=1).reshape(3, *index.shape)
    next_cell = dirs >= 2.0
    next_line = (dirs == 1.0) | (dirs == 3.0)
    line = index + jnp.where(next_line, side, -side)
    step = jnp.where(next_cell, 1, -1)
    place = index % side + step
    line_ok = (line >= 0) & (line < total)
    cell_ok = (place >= 0) & (place < side)
    indices = [index, jnp.clip(line, 0, total - 1), jnp.clip(index + step, 0, total - 1)]
    values = [
        value * (1.0 - frac_a - frac_b),
        jnp.where(line_ok, value * frac_a, 0.0),
        jnp.where(cell_ok, value * frac_b, 0.0),
    ]
    return jnp.concatenate(indices), jnp.concatenate(values)


def dense(terms, start, count):
    cells = start + jnp.arange(count)[:, None]
    indices, values = terms
    return sum(
        jnp.where(cells == indices[i][None], values[i][None], 0.0) for i in range(len(indices))
    )


def shards(covariance, courant, upwind, observed, noise):
    row_count, col_count = covariance.shape
    row_size, col_size = lax.axis_size("row"), lax.axis_size("col")
    row_pos, col_pos = lax.axis_index("row"), lax.axis_index("col")
    row_start, col_start = row_pos * row_count, col_pos * col_count
    side = math.isqrt(upwind.shape[0])
    coefs = stencil_coefs(courant, upwind, side)
    row_coefs = lax.dynamic_slice_in_dim(coefs, row_start, row_count + 2 * side, 1)
    col_coefs = lax.dynamic_slice_in_dim(coefs, col_start, col_count + 2 * side, 1)

    forward = [(i, i + 1) for i in range(row_size - 1)]
    backward = [(target, source) for source, target in forward]
    low = lax.ppermute(covariance[row_count - 2 * side :], "row", forward)

    table = jnp.concatenate([courant, upwind.astype(jnp.float32)[None]])
    depth = observed.shape[1]
    indices, values = expand(
        observed.reshape(1, -1), jnp.ones_like(noise).reshape(1, -1), table, side
    )
    one = indices[:, :depth], values[:, :depth]
    two = expand(indices[:, depth:], values[:, depth:], table, side)

    def observing(start, count):
        return jnp.concatenate([dense(one, start, count), dense(two, start, count)], axis=1)

    part = jnp.dot(covariance, observing(col_start, col_count), precision=HIGHEST)
    part, low, first_lines = lax.optimization_barrier((part, low, covariance[: 2 * side]))
    high = lax.ppermute(first_lines, "row", backward)
    chunk = lax.psum_scatter(part, "col", scatter_dimension=0, tiled=True)
    chunk_count = chunk.shape[0]
    mine = observing(row_start + col_pos * chunk_count, chunk_count)
    innov = lax.psum(jnp.dot(mine.T, chunk, precision=HIGHEST), ("row", "col"))
    innov = innov + jnp.diag(noise.reshape(-1))

    moves = []
    for source in range(row_size * col_size):
        moves.append((source, source % row_size * col_size + source // row_size))
    col_chunk = lax.ppermute(chunk, ("row", "col"), moves)
    row_panel = lax.all_gather(chunk, "col", axis=0, tiled=True)

    unit = jnp.eye(depth, dtype=innov.dtype)
    first_factor = jnp.linalg.cholesky(innov[:depth, :depth])
    first = jax.scipy.linalg.solve_triangular(first_factor, unit, lower=True)
    first, col_chunk = lax.optimization_barrier((first, col_chunk))
    col_panel = lax.all_gather(col_chunk, "row", axis=0, tiled=True)
    cross = jnp.dot(innov[depth:, :depth], first.T, precision=HIGHEST)
    rest = innov[depth:, depth:] - jnp.dot(cross, cross.T, precision=HIGHEST)
    factor, high = lax.optimization_barrier((jnp.linalg.cholesky(rest), high))
    block = left_twice(low, covariance, high, row_coefs, side)
    factor, block = lax.optimization_barrier((factor, block))
    low, high = shifted(block, "col", 1, 2 * side)
    second = jax.scipy.linalg.solve_triangular(factor, unit, lower=True)
    across = jnp.dot(second, jnp.dot(cross, first, precision=HIGHEST), precision=HIGHEST)
    inverse = jnp.concatenate(
        [
            jnp.concatenate([first, jnp.zeros_like(first)], axis=1),
            jnp.concatenate([-across, second], axis=1),
        ]
    )
    inverse, low, high = lax.optimization_barrier((inverse, low, high))
    row_ends = shifted(row_panel, "row", 0, 2 * side)
    col_ends = shifted(col_panel, "col", 0, 2 * side)
    block = right_twice(low, block, high, col_coefs, side)
    block, row_ends, col_ends = lax.optimization_barrier((block, row_ends, col_ends))
    row_panel = left_twice(row_ends[0], row_panel, row_ends[1], row_coefs, side)
    col_panel = left_twice(col_ends[0], col_panel, col_ends[1], col_coefs, side)
    row_panel = jnp.dot(row_panel, inverse.T, precision=HIGHEST)
    col_panel = lax.dot_general(
        inverse, col_panel, (((1,), (1,)), ((), ())), precision=HIGHEST
    )
    return subtract_product(block, row_panel, col_panel)


def solution(mesh):
    in_specs = (P("row", "col"), P(), P(), P(), P())
    out_specs = P("row", "col")
    return jax.shard_map(shards, mesh=mesh, in_specs=in_specs, out_specs=out_specs, check_vma=False)
```
